512 devices in a mesh: ctx: 32 (over z_lo, x, core), exp: 16 (over y, z_hi).
Axes of the slice: x: 4, y: 8, z: 8 (z_hi: 2, z_lo: 4; z = z_hi * 4 + z_lo), core: 2. Of those that a mesh axis runs over, the one named last changes fastest.
Arguments:
- tokens: bfloat16 [8192, 7168], P('ctx', 'exp'), may hold values from -6 to 6
- shared_gate: bfloat16 [7168, 2048], P('ctx', 'exp'), may hold values from -0.0625 to 0.0625
- shared_up: bfloat16 [7168, 2048], P('ctx', 'exp'), may hold values from -0.0625 to 0.0625
- shared_down: bfloat16 [2048, 7168], P(None, 'exp'), may hold values from -0.125 to 0.125
- expert_gate: bfloat16 [16, 7168, 2048], P('exp', 'ctx'), may hold values from -0.0625 to 0.0625
- expert_up: bfloat16 [16, 7168, 2048], P('exp', 'ctx'), may hold values from -0.0625 to 0.0625
- expert_down: bfloat16 [16, 2048, 7168], P('exp', None, 'ctx'), may hold values from -0.125 to 0.125
- hit_rows: int32 [32, 16, 6], P('ctx'), may hold values from 0 to 255, as said below
- hit_counts: int32 [32, 16], P('ctx'), may hold values from 1 to 6, 48 in all within a row
- hit_weights: float32 [32, 16, 6], P('ctx'), may hold values from 0.1 to 1
Outputs:
- mixed: bfloat16 [8192, 7168], P('ctx', 'exp')
The draws below stay inside these ranges and needn't reach their ends.
Inputs may be any that keep to these rules, and one draw needn't show every extreme that they name: `hit_rows`: the 6 entries of one ctx shard and one expert are distinct token positions of that shard; entries from the shard's count on are to be ignored. `hit_counts`: the counts of one ctx shard add up to exactly 48, and the largest count of every ctx shard is 6.
All inputs are finite; a program needn't handle non-finite values.
Results may differ from the reference program's by a relative error of at most 0.022.
Values may be sent and summed in bfloat16 or wider, within the bound.
No kernel may reach another device: no remote copies, remote signals or barrier semaphores. Data moves between devices by JAX's collectives and lax.ppermute only.
A program may use at most 64 MiB of HBM per device.

```python
import math
import jax
import jax.numpy as jnp
import numpy as np
from jax import lax

D = 7168
FF = 2048
FS = 2048
TOK_CTX = 256
CAP = 6
EXPERTS = 16
LIVE = 48
TOKENS = 8192
N_CTX = 32


def draw_hit_rows(key, part):
    key = jax.random.fold_in(key, 11)
    keys = jax.random.split(key, N_CTX * EXPERTS)
    lists = jax.vmap(lambda single: jax.random.permutation(single, TOK_CTX)[:CAP])(keys)
    return lists.reshape(N_CTX, EXPERTS, CAP).astype(jnp.int32)


def block_levels(own_key, extent, pieces, least, top_value):
    def one(dim, shards_of):
        steps = jax.random.uniform(jax.random.fold_in(jax.random.fold_in(own_key, 6), dim), (shards_of,), jnp.float32, least / len(pieces), top_value / len(pieces))
        return jnp.repeat(jnp.exp(steps), extent[dim] // shards_of).reshape((-1,) + (1,) * (len(extent) - dim - 1))

    gain = one(*pieces[0])
    for cut in pieces[1:]:
        gain = gain * one(*cut)
    return gain


def split_up(count, total, most, skew):
    portions = [(1 << 20) // math.isqrt(standing ** skew) + 1 for standing in range(2, count + 1)]
    rest, given = total - most - (count - 1), [1] * (count - 1)
    while rest > 0:
        candidates = [i for i in range(count - 1) if given[i] < most]
        whole, budget = sum([portions[i] for i in candidates]), rest
        for i in candidates:
            addition = min(most - given[i], max(1, budget * portions[i] // whole), rest)
            given[i] = given[i] + addition
            rest = rest - addition
    return np.array([most] + given)


def uneven(stream_key, count, total, reach, lean):
    if count == 2:
        one = jax.random.randint(stream_key, (), max(1, total - reach), min(reach, total - 1) + 1)
        return jnp.stack([one, total - one])
    lengths = jnp.asarray(split_up(count, total, reach, lean), jnp.int32)
    pairs = (count - 1) // 2
    donor, receiver = lengths[1:1 + 2 * pairs:2], lengths[2:2 + 2 * pairs:2]
    margin = jnp.minimum(donor - 1, reach - receiver)
    moved = jax.random.randint(jax.random.fold_in(stream_key, 1), (pairs,), 0, 1 << 20) % (margin + 1)
    lengths = lengths.at[1:1 + 2 * pairs:2].set(donor - moved).at[2:2 + 2 * pairs:2].set(receiver + moved)
    return lengths[jax.random.permutation(jax.random.fold_in(stream_key, 2), count)]


def bell_draw(own_key, shape, scale, reach, cuts=(), held_as=jnp.bfloat16):
    level = block_levels(own_key, shape, cuts, -0.22, 0.18) if cuts else 1.0
    result = jax.random.normal(own_key, shape, jnp.float32) * scale * level
    return jnp.minimum(jnp.maximum(result, -reach), reach).astype(held_as)


def setup_inputs(seed: int = 0) -> dict:
    arg_keys = jax.random.split(jax.random.key(seed), 11)
    tokens = bell_draw(arg_keys[0], (TOKENS, D), 1.0, 6.0, ((0, 32), (1, 16)))
    shared_gate = bell_draw(arg_keys[1], (D, FS), D ** -0.5, 0.0625, ((0, 32), (1, 16)))
    shared_up = bell_draw(arg_keys[2], (D, FS), D ** -0.5, 0.0625, ((0, 32), (1, 16)))
    shared_down = bell_draw(arg_keys[3], (FS, D), FS ** -0.5, 0.125, ((1, 16),))
    expert_gate = bell_draw(arg_keys[4], (EXPERTS, D, FF), D ** -0.5, 0.0625, ((0, 16), (1, 32)))
    expert_up = bell_draw(arg_keys[5], (EXPERTS, D, FF), D ** -0.5, 0.0625, ((0, 16), (1, 32)))
    expert_down = bell_draw(arg_keys[6], (EXPERTS, FF, D), FF ** -0.5, 0.125, ((0, 16), (2, 32)))
    hit_rows = draw_hit_rows(jax.random.fold_in(arg_keys[10], 71), 0)
    hit_counts = jax.vmap(lambda own: uneven(own, EXPERTS, LIVE, CAP, 2))(jax.random.split(arg_keys[8], N_CTX)).reshape((N_CTX, EXPERTS)).astype(jnp.int32)
    hit_weights = jnp.clip(jnp.exp(math.log(1.0) - 2.3025851 * jax.random.uniform(arg_keys[9], (N_CTX, EXPERTS, CAP), jnp.float32) ** block_levels(arg_keys[9], (N_CTX, EXPERTS, CAP), ((0, 32),), -0.2, 0.2)), 0.1, 1.0)
    return dict(tokens=tokens, shared_gate=shared_gate, shared_up=shared_up, shared_down=shared_down, expert_gate=expert_gate, expert_up=expert_up, expert_down=expert_down, hit_rows=hit_rows, hit_counts=hit_counts, hit_weights=hit_weights)


def reference(tokens, shared_gate, shared_up, shared_down, expert_gate, expert_up, expert_down, hit_rows, hit_counts, hit_weights):
    shared_hidden = (jax.nn.silu(jnp.dot(tokens, shared_gate, preferred_element_type=jnp.float32))
                     * jnp.dot(tokens, shared_up, preferred_element_type=jnp.float32)).astype(jnp.bfloat16)
    offsets = (jnp.arange(N_CTX, dtype=jnp.int32) * TOK_CTX)[:, None, None]
    token_index = (offsets + hit_rows.astype(jnp.int32)).astype(jnp.int32)
    slot_ids = jnp.arange(CAP, dtype=jnp.int32)[None, None, :]
    live = slot_ids < hit_counts.astype(jnp.int32)[:, :, None]
    slot_weight = jnp.where(live, hit_weights, jnp.zeros_like(hit_weights)).astype(jnp.float32)
    block = FS // EXPERTS
    total = jnp.zeros((TOKENS, D), jnp.float32)
    for expert in range(EXPERTS):
        rows = token_index[:, expert, :].reshape(-1)
        picked = tokens[rows]
        gate = jnp.dot(picked, expert_gate[expert], preferred_element_type=jnp.float32)
        upper = jnp.dot(picked, expert_up[expert], preferred_element_type=jnp.float32)
        hidden = (jax.nn.silu(gate) * upper).astype(jnp.bfloat16)
        output = jnp.dot(hidden, expert_down[expert], preferred_element_type=jnp.float32)
        output = output * slot_weight[:, expert, :].reshape(-1)[:, None]
        low = expert * block
        part = jnp.dot(shared_hidden[:, low:low + block], shared_down[low:low + block, :],
                       preferred_element_type=jnp.float32)
        part = part.at[rows].add(output)
        rounded = lax.optimization_barrier(part.astype(jnp.bfloat16))
        total = total + rounded.astype(jnp.float32)
    return total.astype(jnp.bfloat16)
```

```python
import jax
import jax.numpy as jnp
from jax import lax
from jax.experimental import pallas as pl
from jax.experimental.pallas import tpu as pltpu
from jax.sharding import Mesh, PartitionSpec as P

CTX = ("z", "x", "c")
CHIP = ("z", "x")
EXP = ("y", "h")
f32, bf16 = jnp.float32, jnp.bfloat16


def exchange(v, axes):
    return lax.all_to_all(v, axes, 0, 0, tiled=True)


def gather(v, axes, n):
    return exchange(jnp.broadcast_to(v[None], (n,) + v.shape), axes)


def swap(v, axis):
    return lax.ppermute(v, axis, [(0, 1), (1, 0)])


def dot(a, b):
    return jnp.dot(a, b, preferred_element_type=f32)


def in_kernel(tok, own, other, out):
    for f in range(2):
        acc = jnp.zeros((256, 256), f32)
        for z in range(4):
            for a in range(2):
                w = jnp.concatenate([own[2 * a + f, z], other[2 * a + f, z]], axis=0)
                acc += dot(tok[2 * z + a], w)
        out[:, f * 256:(f + 1) * 256] = acc


def out_kernel(hid, down, spread, slots, out):
    acc = dot(spread[...], slots[...])
    for y in range(8):
        acc += dot(hid[y], down[y])
    out[...] = acc.astype(bf16)


def body(tokens, shared_gate, shared_up, shared_down, expert_gate, expert_up,
         expert_down, hit_rows, hit_counts, hit_weights):
    core = lax.axis_index("c")
    half = lax.axis_index("h")
    expert = lax.axis_index(EXP)
    first = core == 0

    ids = hit_rows[0].reshape(96)
    pick = (ids[:, None] == jnp.arange(256, dtype=jnp.int32)[None, :]).astype(bf16)
    picked = dot(pick, tokens).astype(bf16).reshape(16, 6, 448)
    mine = exchange(picked, EXP)
    both = jnp.stack([mine, jnp.roll(mine, 224, axis=-1)], axis=1).reshape(32, 6, 448)
    arrived = exchange(both, CTX).reshape(192, 448)

    def halves(w, axis):
        lo, hi = jnp.split(w, 2, axis=axis)
        return jnp.where(first, lo, hi), jnp.where(first, hi, lo)

    g_own, g_send = halves(expert_gate[0], 1)
    u_own, u_send = halves(expert_up[0], 1)
    d_own, d_send = halves(expert_down[0], 0)
    g_w = jnp.concatenate([g_own, swap(g_send, "c")], axis=0)
    u_w = jnp.concatenate([u_own, swap(u_send, "c")], axis=0)
    d_other = swap(d_send, "c")

    g_part = dot(arrived, g_w).astype(bf16).reshape(16, 12, 1024)
    u_part = dot(arrived, u_w).astype(bf16).reshape(16, 12, 1024)
    sums = exchange(jnp.concatenate([g_part, u_part], axis=1), CHIP)
    sums = jnp.sum(sums.astype(f32), axis=0)
    hidden = (jax.nn.silu(sums[:12]) * sums[12:]).astype(bf16)
    hidden = gather(hidden, CHIP, 16).reshape(192, 1024)
    o_own, o_other = dot(hidden, d_own), dot(hidden, d_other)
    o_part = jnp.concatenate(
        [jnp.where(first, o_own, o_other), jnp.where(first, o_other, o_own)], axis=1)
    back = exchange(o_part.astype(bf16).reshape(32, 6, 448), CTX)
    back = jnp.sum(back.astype(f32).reshape(16, 2, 6, 448), axis=1)
    live = jnp.arange(6, dtype=jnp.int32)[None, :] < hit_counts[0][:, None]
    weights = jnp.where(live, hit_weights[0], 0.0)
    weight = lax.dynamic_index_in_dim(weights, expert, 0, keepdims=False)
    back = (back * weight[None, :, None]).astype(bf16)
    slots = exchange(back, EXP).reshape(96, 448)

    tok = jnp.where(first, tokens, jnp.roll(tokens, 224, axis=1))
    tok = gather(tok, "y", 8)
    w = jnp.concatenate([shared_gate, shared_up], axis=1)
    turn = []
    for x in range(4):
        for h in range(2):
            turn.append((2 * x + h, 2 * ((x & 2) | h) + (x & 1)))
    w = lax.ppermute(w, ("x", "h"), turn)
    w = gather(w, "z", 4)
    w = gather(w, "x", 4)
    w_other = swap(w, "c")
    part = pl.pallas_call(
        in_kernel, out_shape=jax.ShapeDtypeStruct((256, 512), f32),
        compiler_params=pltpu.CompilerParams(vmem_limit_bytes=40 << 20),
    )(tok, w, w_other)
    lo, hi = part[:128], part[128:]
    keep = jnp.where(half == 0, lo, hi)
    send = jnp.where(half == 0, hi, lo).astype(bf16)
    total = (keep + swap(send, "h").astype(f32)).reshape(128, 2, 2, 128)
    sh = (jax.nn.silu(total[:, :, 0]) * total[:, :, 1]).astype(bf16).reshape(128, 256)
    sh = gather(sh, EXP, 16).reshape(8, 256, 256)

    spread = (ids[None, :] == jnp.arange(256, dtype=jnp.int32)[:, None]).astype(bf16)
    return pl.pallas_call(
        out_kernel, out_shape=jax.ShapeDtypeStruct((256, 448), bf16),
        compiler_params=pltpu.CompilerParams(vmem_limit_bytes=40 << 20),
    )(sh, shared_down.reshape(8, 256, 448), spread, slots)


def solution(mesh):
    fine = Mesh(mesh.devices.reshape(4, 4, 2, 8, 2), ("z", "x", "c", "y", "h"))
    placed = (
        P(CTX, EXP),
        P(CTX, EXP),
        P(CTX, EXP),
        P(None, EXP),
        P(EXP, CTX, None),
        P(EXP, CTX, None),
        P(EXP, None, CTX),
        P(CTX, None, None),
        P(CTX, None),
        P(CTX, None, None),
    )
    return jax.shard_map(
        body, mesh=fine, in_specs=placed, out_specs=P(CTX, EXP), check_vma=False)
```

```python
import jax
import jax.numpy as jnp
from jax import lax
from jax.experimental import pallas as pl
from jax.experimental.pallas import tpu as pltpu
from jax.sharding import Mesh, PartitionSpec as P

CTX = ("z", "x", "c")
CHIP = ("z", "x")
EXP = ("y", "h")
f32, bf16 = jnp.float32, jnp.bfloat16
VMEM = pltpu.CompilerParams(vmem_limit_bytes=40 << 20)


def exchange(v, axes):
    return lax.all_to_all(v, axes, 0, 0, tiled=True)


def gather(v, axes, n):
    return exchange(jnp.broadcast_to(v[None], (n,) + v.shape), axes)


def swap(v, axis):
    return lax.ppermute(v, axis, [(0, 1), (1, 0)])


def dot(a, b):
    return jnp.dot(a, b, preferred_element_type=f32)


def dot_t(a, b):
    return lax.dot_general(a, b, (((1,), (1,)), ((), ())), preferred_element_type=f32)


def call(kernel, shapes, *args, scalars=0, after=()):
    specs = [pl.BlockSpec(memory_space=pltpu.SMEM)] * scalars
    specs += [pl.BlockSpec(memory_space=pltpu.VMEM)] * (len(args) - scalars)
    specs += [pl.BlockSpec(memory_space=pl.ANY)] * len(after)
    count = len(args)

    def run(*refs):
        kernel(*refs[:count], *refs[count + len(after):])

    return pl.pallas_call(
        run, out_shape=[jax.ShapeDtypeStruct(*v) for v in shapes], in_specs=specs,
        compiler_params=VMEM)(*args, *after)


def stack_kernel(*refs):
    out = refs[-1]
    size = refs[0].shape[0]
    for i, ref in enumerate(refs[:-1]):
        out[i * size:(i + 1) * size] = ref[...]


def pick_kernel(spread, tokens_t, out):
    out[...] = dot_t(spread[...], tokens_t[...]).astype(bf16)


def double_kernel(rows, out):
    out[:, 0] = rows[...]
    out[:, 1] = rows[...]


def expert_kernel(rows, gate, up, out):
    to = lax.broadcasted_iota(jnp.int32, (384, 256), 0)
    at = lax.broadcasted_iota(jnp.int32, (384, 256), 1)
    row = to % 24 % 12
    hit = at == to // 24 * 16 + row // 6 * 8 + row % 6
    g = dot(rows[...], gate[...]).astype(bf16)
    u = dot(rows[...], up[...]).astype(bf16)
    is_gate = to % 24 < 12
    both = dot((hit & is_gate).astype(f32).astype(bf16), g)
    both += dot((hit & ~is_gate).astype(f32).astype(bf16), u)
    out[...] = both.astype(bf16)


def hidden_kernel(sums, out):
    total = sums[0].astype(f32)
    for i in range(1, 16):
        total += sums[i].astype(f32)
    g, u = total[:12], total[12:]
    hidden = (g / (1 + jnp.exp(-g)) * u).astype(bf16)
    for i in range(16):
        out[i] = hidden


def in_kernel(place, tok, w0, w1, w2_lo, w2_hi, w3, keep, send):
    z, x = place[0], place[1]

    def rows(s, t):
        if s == 2:
            return (w2_lo, w2_hi)[t // 2][t % 2 * 224:(t % 2 + 1) * 224]
        return (w0, w1, None, w3)[s][t * 224:(t + 1) * 224]

    for odd in range(2):
        acc = jnp.zeros((512, 256), f32)
        for s in (odd, odd + 2):
            a = ((x + 4 - s) % 4) // 2
            for t in range(4):
                acc += dot(tok[2 * ((z + 4 - t) % 4) + a][:, :224], rows(s, t))
        f = (x + odd) % 2
        cols = pl.ds(pl.multiple_of(f * 256, 256), 256)
        keep[:, cols] = acc[:256]
        send[:, cols] = acc[256:].astype(bf16)


def out_kernel(hid, down, spread, slots, out):
    acc = lax.dot_general(slots[...], spread[...], (((0,), (0,)), ((), ())),
                          preferred_element_type=f32)
    for y in range(8):
        acc += dot_t(down[:, y * 256:(y + 1) * 256], hid[y])
    out[...] = acc.astype(bf16)


def body(tokens, shared_gate, shared_up, shared_down, expert_gate, expert_up,
         expert_down, hit_rows, hit_counts, hit_weights):
    core = lax.axis_index("c")
    expert = lax.axis_index(EXP)
    x, z = lax.axis_index("x"), lax.axis_index("z")
    first = core == 0

    lo, hi = tokens[:, :224], tokens[:, 224:]
    tok_own = jnp.pad(jnp.where(first, lo, hi), ((0, 0), (0, 32)))
    tok_other = swap(jnp.pad(jnp.where(first, hi, lo), ((0, 0), (0, 32))), "c")
    w = jnp.concatenate([shared_gate, shared_up], axis=1)
    pieces = []
    for s in range(4):
        turn = []
        for k in range(4):
            for i in range(4):
                for j in range(2):
                    turn.append((8 * k + 2 * i + j,
                                 8 * ((k + s) % 4) + 2 * ((i & 2) | j) + (i & 1)))
        pieces.append(lax.ppermute(w, ("z", "x", "h"), turn))

    def chip_rows(v):
        lo, hi = v[:, :1024], v[:, 1024:]
        own = jnp.where(first, lo, hi)
        got = swap(jnp.where(first, hi, lo), "c")
        return jnp.concatenate(
            [jnp.where(first, own, got), jnp.where(first, got, own)], axis=0)

    g_w, u_w = chip_rows(expert_gate[0]), chip_rows(expert_up[0])
    d_w = chip_rows(expert_down[0].T)

    ids = jnp.pad(hit_rows[0], ((0, 0), (0, 2)), constant_values=-1).reshape(128)
    spread = (ids[:, None] == jnp.arange(256, dtype=jnp.int32)[None, :]).astype(bf16)
    picked = call(pick_kernel, [((128, 448), bf16)], spread, tokens.T)[0].reshape(16, 8, 448)
    mine = exchange(picked, EXP)
    tok = call(stack_kernel, [((512, 256), bf16)], tok_own, tok_other)[0]
    tok = lax.all_gather(tok, "y", axis=0, tiled=True).reshape(8, 512, 256)
    w = call(stack_kernel, [((896, 256), bf16)], *pieces)[0]
    both = call(double_kernel, [((16, 2, 8, 448), bf16)], mine)[0]
    left = lax.ppermute(w, "x", [(i, (i + 1) % 4) for i in range(4)])
    right = lax.ppermute(w, "x", [(i, (i + 3) % 4) for i in range(4)])
    arrived = exchange(both.reshape(32, 8, 448), CTX).reshape(256, 448)
    far = [lax.ppermute(left[:448], "x", [(i, (i + 1) % 4) for i in range(4)]),
           lax.ppermute(right[448:], "x", [(i, (i + 3) % 4) for i in range(4)])]

    parts = call(expert_kernel, [((384, 1024), bf16)], arrived, g_w, u_w,
                 after=[left, right])[0].reshape(16, 24, 1024)
    sums = exchange(parts, CHIP)
    place = jnp.stack([z, x]).astype(jnp.int32)
    part, send = call(in_kernel, [((256, 512), f32), ((256, 512), bf16)],
                      place, tok, w, left, *far, right, scalars=1, after=[parts])
    part = part + swap(send, "c").astype(f32)
    part = part + swap(part.astype(bf16), "h").astype(f32)
    sh = jnp.concatenate(
        [jax.nn.silu(part[:, i:i + 128]) * part[:, i + 128:i + 256] for i in (0, 256)], axis=1)
    sh = lax.all_gather(sh.astype(bf16), "y", axis=0, tiled=True).reshape(8, 256, 256)

    hidden = call(hidden_kernel, [((16, 12, 1024), bf16)], sums)[0]
    hidden = exchange(hidden, CHIP).reshape(192, 1024)
    back = dot_t(hidden, d_w).astype(bf16).reshape(32, 6, 448)
    back = exchange(jnp.pad(back, ((0, 0), (0, 2), (0, 0))), CTX)
    back = jnp.sum(back.astype(f32).reshape(16, 2, 8, 448), axis=1)
    live = jnp.arange(6, dtype=jnp.int32)[None, :] < hit_counts[0][:, None]
    weights = jnp.pad(jnp.where(live, hit_weights[0], 0.0), ((0, 0), (0, 2)))
    weight = lax.dynamic_index_in_dim(weights, expert, 0, keepdims=False)
    back = (back * weight[None, :, None]).astype(bf16)
    slots = exchange(back, EXP).reshape(128, 448)

    out = pl.pallas_call(
        out_kernel, out_shape=jax.ShapeDtypeStruct((448, 256), bf16),
        compiler_params=VMEM,
    )(sh, shared_down.T, spread, slots)
    return out.T


def solution(mesh):
    fine = Mesh(mesh.devices.reshape(4, 4, 2, 8, 2), ("z", "x", "c", "y", "h"))
    placed = (
        P(CTX, EXP),
        P(CTX, EXP),
        P(CTX, EXP),
        P(None, EXP),
        P(EXP, CTX, None),
        P(EXP, CTX, None),
        P(EXP, None, CTX),
        P(CTX, None, None),
        P(CTX, None),
        P(CTX, None, None),
    )
    return jax.shard_map(
        body, mesh=fine, in_specs=placed, out_specs=P(CTX, EXP), check_vma=False)
```

```python
import jax
import jax.numpy as jnp
from jax import lax
from jax.experimental import pallas as pl
from jax.experimental.pallas import tpu as pltpu
from jax.sharding import Mesh, PartitionSpec as P

CTX = ("z", "x", "c")
CHIP = ("z", "x")
EXP = ("y", "h")
f32, bf16 = jnp.float32, jnp.bfloat16
VMEM = pltpu.CompilerParams(vmem_limit_bytes=40 << 20)


def exchange(v, axes):
    return lax.all_to_all(v, axes, 0, 0, tiled=True)


def gather(v, axes, n):
    return exchange(jnp.broadcast_to(v[None], (n,) + v.shape), axes)


def swap(v, axis):
    return lax.ppermute(v, axis, [(0, 1), (1, 0)])


def dot(a, b):
    return jnp.dot(a, b, preferred_element_type=f32)


def dot_t(a, b):
    return lax.dot_general(a, b, (((1,), (1,)), ((), ())), preferred_element_type=f32)


def call(kernel, shapes, *args, scalars=0, after=()):
    specs = [pl.BlockSpec(memory_space=pltpu.SMEM)] * scalars
    specs += [pl.BlockSpec(memory_space=pltpu.VMEM)] * (len(args) - scalars)
    specs += [pl.BlockSpec(memory_space=pl.ANY)] * len(after)
    count = len(args)

    def run(*refs):
        kernel(*refs[:count], *refs[count + len(after):])

    return pl.pallas_call(
        run, out_shape=[jax.ShapeDtypeStruct(*v) for v in shapes], in_specs=specs,
        compiler_params=VMEM)(*args, *after)


def stack_kernel(*refs):
    out = refs[-1]
    size = refs[0].shape[0]
    for i, ref in enumerate(refs[:-1]):
        out[i * size:(i + 1) * size] = ref[...]


def pick_kernel(spread, tokens_t, out):
    out[...] = dot_t(spread[...], tokens_t[...]).astype(bf16)


def double_kernel(rows, out):
    out[:, 0] = rows[...]
    out[:, 1] = rows[...]


def expert_kernel(rows, gate, up, out):
    to = lax.broadcasted_iota(jnp.int32, (384, 256), 0)
    at = lax.broadcasted_iota(jnp.int32, (384, 256), 1)
    row = to % 24 % 12
    hit = at == to // 24 * 16 + row // 6 * 8 + row % 6
    g = dot(rows[...], gate[...]).astype(bf16)
    u = dot(rows[...], up[...]).astype(bf16)
    is_gate = to % 24 < 12
    both = dot((hit & is_gate).astype(f32).astype(bf16), g)
    both += dot((hit & ~is_gate).astype(f32).astype(bf16), u)
    out[...] = both.astype(bf16)


def hidden_kernel(sums, out):
    total = sums[0].astype(f32)
    for i in range(1, 16):
        total += sums[i].astype(f32)
    g, u = total[:12], total[12:]
    hidden = (g / (1 + jnp.exp(-g)) * u).astype(bf16)
    for i in range(16):
        out[i] = hidden


def in_kernel(place, tok, w0, w1, w2_lo, w2_hi, w3, keep, send):
    z, x = place[0], place[1]

    def rows(s, t):
        if s == 2:
            return (w2_lo, w2_hi)[t // 2][t % 2 * 224:(t % 2 + 1) * 224]
        return (w0, w1, None, w3)[s][t * 224:(t + 1) * 224]

    for odd in range(2):
        acc = jnp.zeros((512, 256), f32)
        for s in (odd, odd + 2):
            a = ((x + 4 - s) % 4) // 2
            for t in range(4):
                acc += dot(tok[2 * ((z + 4 - t) % 4) + a][:, :224], rows(s, t))
        f = (x + odd) % 2
        cols = pl.ds(pl.multiple_of(f * 256, 256), 256)
        keep[:, cols] = acc[:256]
        send[:, cols] = acc[256:].astype(bf16)


def out_kernel(hid, down, spread, slots, out):
    acc = lax.dot_general(slots[...], spread[...], (((0,), (0,)), ((), ())),
                          preferred_element_type=f32)
    for y in range(8):
        acc += dot_t(down[:, y * 256:(y + 1) * 256], hid[y])
    out[...] = acc.astype(bf16)


def body(tokens, shared_gate, shared_up, shared_down, expert_gate, expert_up,
         expert_down, hit_rows, hit_counts, hit_weights):
    core = lax.axis_index("c")
    expert = lax.axis_index(EXP)
    x, z = lax.axis_index("x"), lax.axis_index("z")
    first = core == 0

    lo, hi = tokens[:, :224], tokens[:, 224:]
    tok_own = jnp.pad(jnp.where(first, lo, hi), ((0, 0), (0, 32)))
    tok_other = swap(jnp.pad(jnp.where(first, hi, lo), ((0, 0), (0, 32))), "c")
    w = jnp.concatenate([shared_gate, shared_up], axis=1)
    turn = []
    for i in range(4):
        for j in range(2):
            turn.append((2 * i + j, 2 * ((i & 2) | j) + (i & 1)))
    w = lax.ppermute(w, ("x", "h"), turn)
    pieces = [w] + [lax.ppermute(w, "z", [(i, (i + s) % 4) for i in range(4)]) for s in range(1, 4)]

    def chip_rows(v):
        lo, hi = v[:, :1024], v[:, 1024:]
        own = jnp.where(first, lo, hi)
        got = swap(jnp.where(first, hi, lo), "c")
        return jnp.concatenate(
            [jnp.where(first, own, got), jnp.where(first, got, own)], axis=0)

    g_w, u_w = chip_rows(expert_gate[0]), chip_rows(expert_up[0])
    d_w = chip_rows(expert_down[0].T)

    ids = jnp.pad(hit_rows[0], ((0, 0), (0, 2)), constant_values=-1).reshape(128)
    spread = (ids[:, None] == jnp.arange(256, dtype=jnp.int32)[None, :]).astype(bf16)
    picked = call(pick_kernel, [((128, 448), bf16)], spread, tokens.T)[0].reshape(16, 8, 448)
    mine = exchange(picked, EXP)
    tok = call(stack_kernel, [((512, 256), bf16)], tok_own, tok_other)[0]
    tok = lax.all_gather(tok, "y", axis=0, tiled=True).reshape(8, 512, 256)
    w = call(stack_kernel, [((896, 256), bf16)], *pieces)[0]
    both = call(double_kernel, [((16, 2, 8, 448), bf16)], mine)[0]
    left = lax.ppermute(w, "x", [(i, (i + 1) % 4) for i in range(4)])
    right = lax.ppermute(w, "x", [(i, (i + 3) % 4) for i in range(4)])
    arrived = exchange(both.reshape(32, 8, 448), CTX).reshape(256, 448)
    far = [lax.ppermute(left[:448], "x", [(i, (i + 1) % 4) for i in range(4)]),
           lax.ppermute(right[448:], "x", [(i, (i + 3) % 4) for i in range(4)])]

    parts = call(expert_kernel, [((384, 1024), bf16)], arrived, g_w, u_w,
                 after=[left, right])[0].reshape(16, 24, 1024)
    sums = exchange(parts, CHIP)
    place = jnp.stack([z, x]).astype(jnp.int32)
    part, send = call(in_kernel, [((256, 512), f32), ((256, 512), bf16)],
                      place, tok, w, left, *far, right, scalars=1, after=[parts])
    part = part + swap(send, "c").astype(f32)
    part = part + swap(part.astype(bf16), "h").astype(f32)
    sh = jnp.concatenate(
        [jax.nn.silu(part[:, i:i + 128]) * part[:, i + 128:i + 256] for i in (0, 256)], axis=1)
    sh = lax.all_gather(sh.astype(bf16), "y", axis=0, tiled=True).reshape(8, 256, 256)

    hidden = call(hidden_kernel, [((16, 12, 1024), bf16)], sums)[0]
    hidden = exchange(hidden, CHIP).reshape(192, 1024)
    back = dot_t(hidden, d_w).astype(bf16).reshape(32, 6, 448)
    back = exchange(jnp.pad(back, ((0, 0), (0, 2), (0, 0))), CTX)
    back = jnp.sum(back.astype(f32).reshape(16, 2, 8, 448), axis=1)
    live = jnp.arange(6, dtype=jnp.int32)[None, :] < hit_counts[0][:, None]
    weights = jnp.pad(jnp.where(live, hit_weights[0], 0.0), ((0, 0), (0, 2)))
    weight = lax.dynamic_index_in_dim(weights, expert, 0, keepdims=False)
    back = (back * weight[None, :, None]).astype(bf16)
    slots = exchange(back, EXP).reshape(128, 448)

    out = pl.pallas_call(
        out_kernel, out_shape=jax.ShapeDtypeStruct((448, 256), bf16),
        compiler_params=VMEM,
    )(sh, shared_down.T, spread, slots)
    return out.T


def solution(mesh):
    fine = Mesh(mesh.devices.reshape(4, 4, 2, 8, 2), ("z", "x", "c", "y", "h"))
    placed = (
        P(CTX, EXP),
        P(CTX, EXP),
        P(CTX, EXP),
        P(None, EXP),
        P(EXP, CTX, None),
        P(EXP, CTX, None),
        P(EXP, None, CTX),
        P(CTX, None, None),
        P(CTX, None),
        P(CTX, None, None),
    )
    return jax.shard_map(
        body, mesh=fine, in_specs=placed, out_specs=P(CTX, EXP), check_vma=False)
```

```python
import jax
import jax.numpy as jnp
from jax import lax
from jax.experimental import pallas as pl
from jax.experimental.pallas import tpu as pltpu
from jax.sharding import Mesh, PartitionSpec as P

CTX = ("z", "x", "c")
CHIP = ("z", "x")
EXP = ("y", "h")
f32, bf16 = jnp.float32, jnp.bfloat16
VMEM = pltpu.CompilerParams(vmem_limit_bytes=40 << 20)


def exchange(v, axes):
    return lax.all_to_all(v, axes, 0, 0, tiled=True)


def gather(v, axes, n):
    return exchange(jnp.broadcast_to(v[None], (n,) + v.shape), axes)


def swap(v, axis):
    return lax.ppermute(v, axis, [(0, 1), (1, 0)])


def dot(a, b):
    return jnp.dot(a, b, preferred_element_type=f32)


def dot_t(a, b):
    return lax.dot_general(a, b, (((1,), (1,)), ((), ())), preferred_element_type=f32)


def call(kernel, shapes, *args, scalars=0, after=()):
    specs = [pl.BlockSpec(memory_space=pltpu.SMEM)] * scalars
    specs += [pl.BlockSpec(memory_space=pltpu.VMEM)] * (len(args) - scalars)
    specs += [pl.BlockSpec(memory_space=pl.ANY)] * len(after)
    count = len(args)

    def run(*refs):
        kernel(*refs[:count], *refs[count + len(after):])

    return pl.pallas_call(
        run, out_shape=[jax.ShapeDtypeStruct(*v) for v in shapes], in_specs=specs,
        compiler_params=VMEM)(*args, *after)


def stack_kernel(*refs):
    out = refs[-1]
    size = refs[0].shape[0]
    for i, ref in enumerate(refs[:-1]):
        out[i * size:(i + 1) * size] = ref[...]


def pick_kernel(spread, tokens_t, out):
    out[...] = dot_t(spread[...], tokens_t[...]).astype(bf16)


def halves_kernel(place, rows, own, send):
    for core, out in ((place[0], own), (1 - place[0], send)):
        out[...] = rows[:, pl.ds(pl.multiple_of(core * 1024, 1024), 1024)]


def double_kernel(rows, out):
    out[:, 0] = rows[...]
    out[:, 1] = rows[...]


def expert_kernel(rows, gate, up, out):
    to = lax.broadcasted_iota(jnp.int32, (384, 256), 0)
    at = lax.broadcasted_iota(jnp.int32, (384, 256), 1)
    row = to % 24 % 12
    hit = at == to // 24 * 16 + row // 6 * 8 + row % 6
    g = dot(rows[...], gate[...]).astype(bf16)
    u = dot(rows[...], up[...]).astype(bf16)
    is_gate = to % 24 < 12
    both = dot((hit & is_gate).astype(f32).astype(bf16), g)
    both += dot((hit & ~is_gate).astype(f32).astype(bf16), u)
    out[...] = both.astype(bf16)


def hidden_kernel(sums, out):
    total = sums[0].astype(f32)
    for i in range(1, 16):
        total += sums[i].astype(f32)
    g, u = total[:12], total[12:]
    hidden = (g / (1 + jnp.exp(-g)) * u).astype(bf16)
    for i in range(16):
        out[i] = hidden


def in_kernel(place, tok, w0, w1, w2_lo, w2_hi, w3, keep, send):
    z, x = place[0], place[1]

    def rows(s, t):
        if s == 2:
            return (w2_lo, w2_hi)[t // 2][t % 2 * 224:(t % 2 + 1) * 224]
        return (w0, w1, None, w3)[s][t * 224:(t + 1) * 224]

    for odd in range(2):
        acc = jnp.zeros((512, 256), f32)
        for s in (odd, odd + 2):
            a = ((x + 4 - s) % 4) // 2
            for t in range(4):
                acc += dot(tok[2 * ((z + 4 - t) % 4) + a][:, :224], rows(s, t))
        f = (x + odd) % 2
        cols = pl.ds(pl.multiple_of(f * 256, 256), 256)
        keep[:, cols] = acc[:256]
        send[:, cols] = acc[256:].astype(bf16)


def out_kernel(hid, down, spread, slots, out):
    acc = lax.dot_general(slots[...], spread[...], (((0,), (0,)), ((), ())),
                          preferred_element_type=f32)
    for y in range(8):
        acc += dot_t(down[:, y * 256:(y + 1) * 256], hid[y])
    out[...] = acc.astype(bf16)


def body(tokens, shared_gate, shared_up, shared_down, expert_gate, expert_up,
         expert_down, hit_rows, hit_counts, hit_weights):
    core = lax.axis_index("c")
    expert = lax.axis_index(EXP)
    x, z = lax.axis_index("x"), lax.axis_index("z")
    first = core == 0

    lo, hi = tokens[:, :224], tokens[:, 224:]
    tok_own = jnp.pad(jnp.where(first, lo, hi), ((0, 0), (0, 32)))
    tok_other = swap(jnp.pad(jnp.where(first, hi, lo), ((0, 0), (0, 32))), "c")
    w = jnp.concatenate([shared_gate, shared_up], axis=1)
    turn = []
    for i in range(4):
        for j in range(2):
            turn.append((2 * i + j, 2 * ((i & 2) | j) + (i & 1)))
    w = lax.ppermute(w, ("x", "h"), turn)
    pieces = [w] + [lax.ppermute(w, "z", [(i, (i + s) % 4) for i in range(4)]) for s in range(1, 4)]

    def chip_rows(v):
        lo, hi = v[:, :1024], v[:, 1024:]
        own = jnp.where(first, lo, hi)
        got = swap(jnp.where(first, hi, lo), "c")
        return jnp.concatenate(
            [jnp.where(first, own, got), jnp.where(first, got, own)], axis=0)

    ids = jnp.pad(hit_rows[0], ((0, 0), (0, 2)), constant_values=-1).reshape(128)
    spread = (ids[:, None] == jnp.arange(256, dtype=jnp.int32)[None, :]).astype(bf16)
    picked = call(pick_kernel, [((128, 448), bf16)], spread, tokens.T)[0].reshape(16, 8, 448)
    g_own, g_send = call(halves_kernel, [((224, 1024), bf16)] * 2,
                         core.reshape(1).astype(jnp.int32), expert_gate[0], scalars=1,
                         after=[picked])
    g_got = swap(g_send, "c")
    g_w = jnp.concatenate(
        [jnp.where(first, g_own, g_got), jnp.where(first, g_got, g_own)], axis=0)
    u_w, d_w = chip_rows(expert_up[0]), chip_rows(expert_down[0].T)

    mine = exchange(picked, EXP)
    tok = call(stack_kernel, [((512, 256), bf16)], tok_own, tok_other)[0]
    tok = lax.all_gather(tok, "y", axis=0, tiled=True).reshape(8, 512, 256)
    w = call(stack_kernel, [((896, 256), bf16)], *pieces)[0]
    both = call(double_kernel, [((16, 2, 8, 448), bf16)], mine)[0]
    left = lax.ppermute(w, "x", [(i, (i + 1) % 4) for i in range(4)])
    right = lax.ppermute(w, "x", [(i, (i + 3) % 4) for i in range(4)])
    arrived = exchange(both.reshape(32, 8, 448), CTX).reshape(256, 448)
    far = [lax.ppermute(left[:448], "x", [(i, (i + 1) % 4) for i in range(4)]),
           lax.ppermute(right[448:], "x", [(i, (i + 3) % 4) for i in range(4)])]

    parts = call(expert_kernel, [((384, 1024), bf16)], arrived, g_w, u_w,
                 after=[left, right])[0].reshape(16, 24, 1024)
    sums = exchange(parts, CHIP)
    place = jnp.stack([z, x]).astype(jnp.int32)
    part, send = call(in_kernel, [((256, 512), f32), ((256, 512), bf16)],
                      place, tok, w, left, *far, right, scalars=1, after=[parts])
    part = part + swap(send, "c").astype(f32)
    part = part + swap(part.astype(bf16), "h").astype(f32)
    sh = jnp.concatenate(
        [jax.nn.silu(part[:, i:i + 128]) * part[:, i + 128:i + 256] for i in (0, 256)], axis=1)
    sh = lax.all_gather(sh.astype(bf16), "y", axis=0, tiled=True).reshape(8, 256, 256)

    hidden = call(hidden_kernel, [((16, 12, 1024), bf16)], sums)[0]
    hidden = exchange(hidden, CHIP).reshape(192, 1024)
    back = dot_t(hidden, d_w).astype(bf16).reshape(32, 6, 448)
    back = exchange(jnp.pad(back, ((0, 0), (0, 2), (0, 0))), CTX)
    back = jnp.sum(back.astype(f32).reshape(16, 2, 8, 448), axis=1)
    live = jnp.arange(6, dtype=jnp.int32)[None, :] < hit_counts[0][:, None]
    weights = jnp.pad(jnp.where(live, hit_weights[0], 0.0), ((0, 0), (0, 2)))
    weight = lax.dynamic_index_in_dim(weights, expert, 0, keepdims=False)
    back = (back * weight[None, :, None]).astype(bf16)
    slots = exchange(back, EXP).reshape(128, 448)

    out = pl.pallas_call(
        out_kernel, out_shape=jax.ShapeDtypeStruct((448, 256), bf16),
        compiler_params=VMEM,
    )(sh, shared_down.T, spread, slots)
    return out.T


def solution(mesh):
    fine = Mesh(mesh.devices.reshape(4, 4, 2, 8, 2), ("z", "x", "c", "y", "h"))
    placed = (
        P(CTX, EXP),
        P(CTX, EXP),
        P(CTX, EXP),
        P(None, EXP),
        P(EXP, CTX, None),
        P(EXP, CTX, None),
        P(EXP, None, CTX),
        P(CTX, None, None),
        P(CTX, None),
        P(CTX, None, None),
    )
    return jax.shard_map(
        body, mesh=fine, in_specs=placed, out_specs=P(CTX, EXP), check_vma=False)
```
